32 devices in a mesh: dp: 4 (over y, core), expert: 8 (over z, x).
Axes of the slice: x: 2, y: 2, z: 4, core: 2. Of those that a mesh axis runs over, the one named last changes fastest.
Arguments:
- tokens: bfloat16 [2048, 3584], P('expert', 'dp'), may hold values from -6 to 6
- cotangent: bfloat16 [2048, 3584], P('expert', 'dp'), may hold values from -6 to 6
- slot_tokens: int32 [8, 8, 32], P('expert'), may hold values from 0 to 255
- slot_counts: int32 [8, 8], P('expert'), may hold values from 0 to 32, as said below
- slot_gates: float32 [8, 8, 32], P('expert'), may hold values from 0.1 to 1
- swap_pairs: int32 [4], replicated, may hold values from 0 to 1, as said below
- gate_weight: bfloat16 [8, 3584, 1024], P('expert', 'dp'), may hold values from -0.09375 to 0.09375
- up_weight: bfloat16 [8, 3584, 1024], P('expert', 'dp'), may hold values from -0.09375 to 0.09375
- down_weight: bfloat16 [8, 1024, 3584], P('expert', None, 'dp'), may hold values from -0.1875 to 0.1875
- first_moment: float32 [8, 1024, 3584], P('expert', None, 'dp'), may hold values from -6 to 6
- second_moment: float32 [8, 1024, 3584], P('expert', None, 'dp'), may hold values from 0.5 to 4
Outputs:
- mixed: bfloat16 [2048, 3584], P('expert', 'dp')
- token_grad: bfloat16 [2048, 3584], P('expert', 'dp')
- new_first_moment: float32 [8, 1024, 3584], P('expert', None, 'dp')
- new_second_moment: float32 [8, 1024, 3584], P('expert', None, 'dp')
- adam_step: bfloat16 [8, 1024, 3584], P('expert', None, 'dp')
The draws below stay inside these ranges and needn't reach their ends.
Inputs may be any that keep to these rules, and one draw needn't show every extreme that they name: `slot_tokens`: slots at or past slot_counts hold arbitrary token numbers and carry nothing. `slot_counts`: every source fills all 32 slots of some expert, and one expert receives 32 live slots from every source. `swap_pairs`: at least one pair trades and at least one pair does not.
All inputs are finite; a program needn't handle non-finite values.
Results may differ from the reference program's by a relative error of at most 0.022.
Values may be sent and summed in bfloat16 or wider, within the bound.
A program may use at most 128 MiB of HBM per device.

```python
import math
import jax
import jax.numpy as jnp
from jax import lax

D = 3584
FFW = 1024
CAP = 32
TOK = 256
EXPERTS = 8
N_DP = 4
N_EXPERT = 8


def draw_slot_counts(key, part):
    key_heat, key_fill, key_full, key_pick = jax.random.split(jax.random.fold_in(key, 11), 4)
    heat = jax.random.randint(key_heat, (EXPERTS,), 1, 4)
    ceiling = heat * CAP // 3
    counts = jax.random.randint(key_fill, (EXPERTS, EXPERTS), 0, CAP + 1)
    counts = counts * ceiling[None, :] // CAP
    columns = jnp.arange(EXPERTS)
    full_expert = jax.random.randint(key_full, (), 0, EXPERTS)
    counts = jnp.where(columns[None, :] == full_expert, CAP, counts)
    picked = jax.random.randint(key_pick, (EXPERTS,), 0, EXPERTS)
    counts = jnp.where(columns[None, :] == picked[:, None], CAP, counts)
    return counts.astype(jnp.int32)


def draw_swap_pairs(key, part):
    key_flags, key_force, key_keep = jax.random.split(jax.random.fold_in(key, 23), 3)
    half_count = EXPERTS // 2
    flags = jax.random.randint(key_flags, (half_count,), 0, 2)
    forced = jax.random.randint(key_force, (), 0, half_count)
    offset = jax.random.randint(key_keep, (), 1, half_count)
    kept = (forced + offset) % half_count
    places = jnp.arange(half_count)
    flags = jnp.where(places == forced, 1, flags)
    flags = jnp.where(places == kept, 0, flags)
    return flags.astype(jnp.int32)


def set_ends(entries, own_key, smallest, largest):
    extent = entries.shape
    index_at = [jax.random.randint(jax.random.fold_in(own_key, axis), (), 0, extent[axis]) for axis in range(len(extent))]
    entries = entries.at[tuple(index_at)].set(smallest)
    longest = extent.index(max(extent))
    index_at[longest] = (index_at[longest] + 1) % extent[longest]
    return entries.at[tuple(index_at)].set(largest)


def steps_of(rng, shape, cuts, low, top_value):
    factor_of = 1.0
    for position, shards_of in cuts:
        draws = jax.random.uniform(jax.random.fold_in(jax.random.fold_in(rng, 6), position), (shards_of,), jnp.float32, low / len(cuts), top_value / len(cuts))
        factor_of = factor_of * jnp.repeat(jnp.exp(draws), shape[position] // shards_of).reshape((-1,) + (1,) * (len(shape) - 1 - position))
    return factor_of


def gaussian(rng, shape, deviation, bound, pieces=(), held_as=jnp.bfloat16):
    entries = jax.random.normal(rng, shape, jnp.float32) * deviation
    if len(pieces) > 0:
        entries = steps_of(rng, shape, pieces, -0.22, 0.18) * entries
    return jnp.clip(entries, min=-bound, max=bound).astype(held_as)


def setup_inputs(seed: int = 0) -> dict:
    streams_of = jax.random.split(jax.random.key(seed), 12)
    tokens = gaussian(streams_of[0], (N_EXPERT * TOK, D), 1.0, 6.0, ((0, 8), (1, 4)))
    cotangent = gaussian(streams_of[1], (N_EXPERT * TOK, D), 1.0, 6.0, ((0, 8), (1, 4)))
    slot_tokens = set_ends(jax.random.randint(streams_of[2], (N_EXPERT, EXPERTS, CAP), 0, TOK), jax.random.fold_in(streams_of[2], 1), 0, TOK - 1).astype(jnp.int32)
    slot_counts = draw_slot_counts(jax.random.fold_in(streams_of[11], 71), 0)
    slot_gates = jnp.clip(0.1 + 0.9 * jax.random.uniform(streams_of[4], (N_EXPERT, EXPERTS, CAP), jnp.float32) ** steps_of(streams_of[4], (N_EXPERT, EXPERTS, CAP), ((0, 8),), -0.2, 0.2), 0.1, 1.0)
    swap_pairs = draw_swap_pairs(jax.random.fold_in(streams_of[11], 71), 0)
    gate_weight = gaussian(streams_of[6], (EXPERTS, D, FFW), D ** -0.5, 0.09375, ((0, 8), (1, 4)))
    up_weight = gaussian(streams_of[7], (EXPERTS, D, FFW), D ** -0.5, 0.09375, ((0, 8), (1, 4)))
    down_weight = gaussian(streams_of[8], (EXPERTS, FFW, D), FFW ** -0.5, 0.1875, ((0, 8), (2, 4)))
    first_moment = gaussian(streams_of[9], (EXPERTS, FFW, D), 1.0, 6.0, ((0, 8), (2, 4)), jnp.float32)
    second_moment = jnp.clip(jnp.exp(math.log(4.0) - 2.0794415 * jax.random.uniform(streams_of[10], (EXPERTS, FFW, D), jnp.float32) ** steps_of(streams_of[10], (EXPERTS, FFW, D), ((0, 8), (2, 4)), -0.2, 0.2)), 0.5, 4.0)
    return dict(tokens=tokens, cotangent=cotangent, slot_tokens=slot_tokens, slot_counts=slot_counts, slot_gates=slot_gates, swap_pairs=swap_pairs, gate_weight=gate_weight, up_weight=up_weight, down_weight=down_weight, first_moment=first_moment, second_moment=second_moment)


def held_order(values, pair_flags):
    half_count = pair_flags.shape[0]
    blocks = values.reshape((2, half_count) + values.shape[1:])
    chosen = pair_flags.reshape((1, half_count) + (1,) * (values.ndim - 1)) > 0
    return jnp.where(chosen, blocks[::-1], blocks).reshape(values.shape)

def pick_rows(anchor, positions):
    return anchor[positions]

def reference(tokens, cotangent, slot_tokens, slot_counts, slot_gates, swap_pairs, gate_weight, up_weight, down_weight, first_moment, second_moment):
    block_cols = D // N_DP
    row_count = N_EXPERT * CAP
    live_slots = (jnp.arange(CAP)[None, None, :] < slot_counts[:, :, None]).astype(jnp.float32)
    weighted = live_slots * slot_gates
    token_blocks = tokens.reshape(N_EXPERT, TOK, D)
    grad_blocks = cotangent.reshape(N_EXPERT, TOK, D)
    picked = jax.vmap(pick_rows)(token_blocks, slot_tokens)
    picked = jnp.where(live_slots[..., None] > 0, picked, jnp.zeros_like(picked))
    picked_grad = (jax.vmap(pick_rows)(grad_blocks, slot_tokens).astype(jnp.float32) * weighted[..., None]).astype(jnp.bfloat16)
    by_expert = jnp.swapaxes(picked, 0, 1)
    grad_by_expert = jnp.swapaxes(picked_grad, 0, 1)

    def expert_pass(operands):
        rows_in, grads_in, gate_w, up_w, down_w, moment_one, moment_two = operands
        flat_rows = rows_in.reshape(row_count, D)
        gate_up = jnp.concatenate([gate_w, up_w], axis=1)
        partial_pre = jnp.einsum('rkd,kdf->krf', flat_rows.reshape(row_count, N_DP, block_cols).astype(jnp.float32), gate_up.reshape(N_DP, block_cols, 2 * FFW).astype(jnp.float32))
        preact = lax.optimization_barrier(jnp.sum(lax.optimization_barrier(partial_pre.astype(jnp.bfloat16)).astype(jnp.float32), axis=0))
        gate_pre = preact[:, :FFW]
        up_pre = preact[:, FFW:]
        hidden = (jax.nn.silu(gate_pre) * up_pre).astype(jnp.bfloat16)
        outputs = jnp.dot(hidden, down_w, preferred_element_type=jnp.float32).astype(jnp.bfloat16)
        flat_grad = grads_in.reshape(row_count, D)
        weight_grad = jnp.dot(hidden.T, flat_grad, preferred_element_type=jnp.float32)
        partial_hidden = jnp.einsum('rkd,fkd->krf', flat_grad.reshape(row_count, N_DP, block_cols).astype(jnp.float32), down_w.reshape(FFW, N_DP, block_cols).astype(jnp.float32))
        hidden_grad = lax.optimization_barrier(jnp.sum(lax.optimization_barrier(partial_hidden.astype(jnp.bfloat16)).astype(jnp.float32), axis=0))
        sigmoid_gate = jax.nn.sigmoid(gate_pre)
        preact_grad = jnp.concatenate([hidden_grad * up_pre * sigmoid_gate * (1.0 + gate_pre * (1.0 - sigmoid_gate)), hidden_grad * gate_pre * sigmoid_gate], axis=1).astype(jnp.bfloat16)
        input_grad = jnp.dot(preact_grad, gate_up.T, preferred_element_type=jnp.float32).astype(jnp.bfloat16)
        new_one = 0.9 * moment_one + 0.1 * weight_grad
        new_two = 0.999 * moment_two + 0.001 * weight_grad * weight_grad
        step_dir = (new_one / (jnp.sqrt(new_two) + 1e-08)).astype(jnp.bfloat16)
        return (outputs.reshape(N_EXPERT, CAP, D), input_grad.reshape(N_EXPERT, CAP, D), new_one, new_two, step_dir)
    outputs, input_grads, new_one, new_two, step_dir = lax.map(expert_pass, (by_expert, grad_by_expert, gate_weight, up_weight, down_weight, first_moment, second_moment))

    def combine(slot_values, positions, coef):
        return jnp.zeros((TOK, D), jnp.float32).at[positions.reshape(-1)].add(slot_values.reshape(-1, D).astype(jnp.float32) * coef.reshape(-1, 1))
    mixed = jax.vmap(combine)(jnp.swapaxes(outputs, 0, 1), slot_tokens, weighted).reshape(N_EXPERT * TOK, D).astype(jnp.bfloat16)
    token_grad = jax.vmap(combine)(jnp.swapaxes(input_grads, 0, 1), slot_tokens, live_slots).reshape(N_EXPERT * TOK, D).astype(jnp.bfloat16)
    return (mixed, token_grad, held_order(new_one, swap_pairs), held_order(new_two, swap_pairs), held_order(step_dir, swap_pairs))
```

```python
import functools

import jax
import jax.numpy as jnp
from jax import lax
from jax.sharding import PartitionSpec as P

beta_first = 0.9
beta_second = 0.999
adam_eps = 1e-08


def preact_grad(hidden_grad, gate_pre, up_pre):
    sigmoid_gate = jax.nn.sigmoid(gate_pre)
    first_half = hidden_grad * up_pre * sigmoid_gate * (1.0 + gate_pre * (1.0 - sigmoid_gate))
    second_half = hidden_grad * gate_pre * sigmoid_gate
    return jnp.concatenate([first_half, second_half], axis=1).astype(jnp.bfloat16)


def dp_sum(block):
    size = lax.axis_size("dp")
    if size & (size - 1) or size < 2:
        return lax.psum(block, "dp").astype(jnp.float32)

    def trade(values, bit):
        return lax.ppermute(values, "dp", [(i, i ^ 1 << bit) for i in range(size)])

    upper = lax.axis_index("dp") % 2 == 1
    rows = block.shape[0] // 2
    low, high = block[:rows], block[rows:]
    own = jnp.where(upper, high, low).astype(jnp.float32)
    total = own + trade(jnp.where(upper, low, high), 0).astype(jnp.float32)
    for bit in range(1, size.bit_length() - 1):
        sent = total.astype(jnp.bfloat16)
        total = sent.astype(jnp.float32) + trade(sent, bit).astype(jnp.float32)
    sent = total.astype(jnp.bfloat16)
    other = trade(sent, 0)
    return jnp.concatenate(
        [jnp.where(upper, other, sent), jnp.where(upper, sent, other)], axis=0
    ).astype(jnp.float32)


def all_rows(block):
    return lax.all_to_all(block, "expert", split_axis=0, concat_axis=0, tiled=True).reshape(
        -1, block.shape[-1]
    )


def detours(pairs, half_count, chunks):
    columns = [[p for p in pairs if p % 2 == c] for c in range(2)]
    light, heavy = sorted(columns, key=len)
    if half_count != 4 or len(heavy) == len(light):
        return (), 0
    return tuple(heavy), 2 * chunks * (len(heavy) - len(light)) // (2 * len(heavy))


def straight(block, pairs):
    size = lax.axis_size("expert")
    ends = [e for p in pairs for e in (p, p + size // 2)]
    return lax.ppermute(block, "expert", [(e, (e + size // 2) % size) for e in ends])


def relocate(pairs, chunks, one, two, back_rows):
    size = lax.axis_size("expert")
    around, count = detours(pairs, size // 2, chunks)
    if not around:
        returned_grad = all_rows(back_rows)
        return straight(one, pairs), straight(two, pairs), returned_grad
    rows = one.shape[0] // chunks
    ends = [e for p in around for e in (p, p + size // 2)]
    direct = [p for p in pairs if p not in around]
    beside = [
        lax.ppermute(one[k * rows : (k + 1) * rows], "expert", [(e, e ^ 1) for e in ends])
        for k in range(count)
    ]
    returned_grad = all_rows(back_rows)
    far_two = straight(two, pairs)
    parts = []
    for k in range(count):
        part = lax.ppermute(
            beside[k], "expert", [(e ^ 1, (e + size // 2) % size) for e in ends]
        )
        if direct:
            goes_round = functools.reduce(
                jnp.logical_or, [lax.axis_index("expert") == e for e in ends]
            )
            part = jnp.where(
                goes_round, part, straight(one[k * rows : (k + 1) * rows], direct)
            )
        parts.append((k * rows, part))
    if count < chunks:
        parts.append((count * rows, straight(one[count * rows :], pairs)))
    far_one = jnp.zeros_like(one)
    for start, part in parts:
        far_one = lax.dynamic_update_slice(far_one, part, (start, 0))
    return far_one, far_two, returned_grad


def trade_moments(swap_pairs, one, two, back_rows):
    half_count = swap_pairs.shape[0]
    every = range(half_count)
    if half_count > 4:
        return relocate(tuple(every), 4, one, two, back_rows)
    combos = [
        tuple(p for p in every if code >> p & 1) for code in range(1, (1 << half_count) - 1)
    ]
    code = jnp.sum(swap_pairs << jnp.arange(half_count))
    return lax.switch(
        code - 1,
        [functools.partial(relocate, pairs, 4) for pairs in combos],
        one,
        two,
        back_rows,
    )


def shards(
    tokens,
    cotangent,
    slot_tokens,
    slot_counts,
    slot_gates,
    swap_pairs,
    gate_weight,
    up_weight,
    down_weight,
    first_moment,
    second_moment,
):
    tok_count, model_cols = tokens.shape
    experts = slot_counts.shape[1]
    capacity = slot_tokens.shape[2]
    position = lax.axis_index("expert")
    half_count = swap_pairs.shape[0]
    own_swap = (
        jnp.sum(jnp.where(jnp.arange(half_count) == position % half_count, swap_pairs, 0)) > 0
    )
    live_slots = (
        (jnp.arange(capacity)[None, :] < slot_counts[0][:, None]).astype(jnp.float32).reshape(-1)
    )
    weighted = live_slots * slot_gates[0].reshape(-1)
    slot_route = slot_tokens[0].reshape(-1)
    matcher = (jnp.arange(tok_count)[:, None] == slot_route[None, :]).astype(jnp.float32)
    gate_proj, up_proj, down_proj = gate_weight[0], up_weight[0], down_weight[0]
    moment_one = first_moment[0]
    moment_two = second_moment[0]
    hidden_units = down_proj.shape[0]
    contract_last = (((1,), (1,)), ((), ()))
    contract_first = (((0,), (0,)), ((), ()))

    picked = jnp.take(tokens, slot_route, axis=0)
    outgoing = jnp.where(live_slots[:, None] > 0, picked, jnp.zeros_like(picked)).reshape(
        experts, capacity, model_cols
    )
    arrived = all_rows(outgoing)
    partial = jnp.concatenate(
        [
            jnp.dot(arrived, part, preferred_element_type=jnp.float32).astype(jnp.bfloat16)
            for part in (gate_proj, up_proj)
        ],
        axis=1,
    )
    preact = dp_sum(partial)

    grad_picked = jnp.take(cotangent, slot_route, axis=0).astype(jnp.float32) * weighted[:, None]
    grad_slots = grad_picked.astype(jnp.bfloat16).reshape(experts, capacity, model_cols)
    grad_slots, arrived = lax.optimization_barrier((grad_slots, arrived))
    arrived_grad = all_rows(grad_slots)
    partial_grad = lax.dot_general(
        arrived_grad, down_proj, contract_last, preferred_element_type=jnp.float32
    ).astype(jnp.bfloat16)
    hidden_grad = dp_sum(partial_grad)

    gate_pre = preact[:, :hidden_units]
    up_pre = preact[:, hidden_units:]
    hidden = (jax.nn.silu(gate_pre) * up_pre).astype(jnp.bfloat16)
    outputs = (
        jnp.dot(hidden, down_proj, preferred_element_type=jnp.float32)
        .astype(jnp.bfloat16)
        .reshape(-1, capacity, model_cols)
    )
    returned = all_rows(outputs)
    mixed = jnp.dot(
        (matcher * weighted[None, :]).astype(jnp.bfloat16),
        returned,
        preferred_element_type=jnp.float32,
    ).astype(jnp.bfloat16)

    weight_grad = lax.dot_general(
        hidden, arrived_grad, contract_first, preferred_element_type=jnp.float32
    )
    new_one = beta_first * moment_one + (1.0 - beta_first) * weight_grad
    new_two = beta_second * moment_two + (1.0 - beta_second) * weight_grad * weight_grad

    row_grad = preact_grad(hidden_grad, gate_pre, up_pre)
    back_rows = (
        lax.dot_general(
            row_grad[:, :hidden_units], gate_proj, contract_last, preferred_element_type=jnp.float32
        )
        + lax.dot_general(
            row_grad[:, hidden_units:], up_proj, contract_last, preferred_element_type=jnp.float32
        )
    ).astype(jnp.bfloat16)
    far_one, far_two, returned_grad = trade_moments(
        swap_pairs,
        new_one.astype(jnp.bfloat16),
        new_two.astype(jnp.bfloat16),
        back_rows.reshape(-1, capacity, model_cols),
    )
    token_grad = jnp.dot(
        (matcher * live_slots[None, :]).astype(jnp.bfloat16),
        returned_grad,
        preferred_element_type=jnp.float32,
    ).astype(jnp.bfloat16)
    new_one = jnp.where(own_swap, far_one.astype(jnp.float32), new_one)
    new_two = jnp.where(own_swap, far_two.astype(jnp.float32), new_two)
    step_dir = (new_one / (jnp.sqrt(new_two) + adam_eps)).astype(jnp.bfloat16)
    return (mixed, token_grad, new_one[None], new_two[None], step_dir[None])


def solution(mesh):
    return jax.shard_map(
        shards,
        mesh=mesh,
        in_specs=(
            P("expert", "dp"),
            P("expert", "dp"),
            P("expert", None, None),
            P("expert", None),
            P("expert", None, None),
            P(),
            P("expert", "dp", None),
            P("expert", "dp", None),
            P("expert", None, "dp"),
            P("expert", None, "dp"),
            P("expert", None, "dp"),
        ),
        out_specs=(
            P("expert", "dp"),
            P("expert", "dp"),
            P("expert", None, "dp"),
            P("expert", None, "dp"),
            P("expert", None, "dp"),
        ),
        check_vma=False,
    )
```
